512 devices in a mesh: section: 16 (over z), peer: 32 (over y, x, core).
Axes of the slice: x: 4, y: 4, z: 16, core: 2. Of those that a mesh axis runs over, the one named last changes fastest.
Arguments:
- emitted: bfloat16 [16, 32, 128, 5120], P('section', 'peer'), may hold values from -6 to 6
- out_grads: bfloat16 [16, 32, 128, 5120], P('section', 'peer'), may hold values from -6 to 6
- adapter_in: bfloat16 [16, 16, 5120], P('section'), may hold values from -0.078125 to 0.078125
- adapter_out: bfloat16 [16, 16, 5120], P('section'), may hold values from -0.375 to 0.375
- wiring: int32 [16, 32, 32, 1], P('section', 'peer'), may hold values from 0 to 31; in each aligned block of 32 rows (0 to 31, 32 to 63, ..., all dimensions but the last counted through in order) no two rows name the same one
- counts: int32 [16, 32], P('section', 'peer'), may hold values from 24 to 32
Outputs:
- row_grads: bfloat16 [16, 32, 128, 5120], P('section', 'peer')
- grad_in: float32 [16, 16, 5120], P('section')
- grad_out: float32 [16, 16, 5120], P('section')
The draws below stay inside these ranges and needn't reach their ends.
Inputs may be any that keep to these rules, and one draw needn't show every extreme that they name: `wiring`: on every peer of every section the 32 blocks name each peer exactly 1 times.
All inputs are finite; a program needn't handle non-finite values.
Results may differ from the reference program's by a relative error of at most 0.0053.
Values may be sent and summed in bfloat16 or wider, within the bound.
No kernel may reach another device: no remote copies, remote signals or barrier semaphores. Data moves between devices by JAX's collectives and lax.ppermute only.
A program may use at most 64 MiB of HBM per device.

```python
import math
import jax
import jax.numpy as jnp
import numpy as np
from jax import lax

D = 5120
RANK = 16
NB = 32
BLK = 4
ROWS = 128
MOST = 1
N_SECTION = 16
N_PEER = 32


def with_ends(result, key, least, largest):
    dims = result.shape
    spot = [jax.random.randint(jax.random.fold_in(key, axis), (), 0, dims[axis]) for axis in range(len(dims))]
    result = result.at[tuple(spot)].set(least)
    longest = dims.index(max(dims))
    spot[longest] = (spot[longest] + 1) % dims[longest]
    return result.at[tuple(spot)].set(largest)


def level_of(key, shape, pieces, least, high):
    loudness = 1.0
    for position, parts in pieces:
        steps = jax.random.uniform(jax.random.fold_in(jax.random.fold_in(key, 6), position), (parts,), jnp.float32, least / len(pieces), high / len(pieces))
        loudness = loudness * jnp.repeat(jnp.exp(steps), shape[position] // parts).reshape((-1,) + (1,) * (len(shape) - 1 - position))
    return loudness


def assign_block(own_key, own, number, rows, number_of, top, reach, skew):
    sequence = jax.random.permutation(own_key, number_of)
    heavy_load, common = portions_of(number_of, rows * top, reach, skew, True), portions_of(number_of, rows * top, reach, skew, False)
    places = jnp.arange(number_of)

    def named(lengths, offset_by):
        used = int((lengths > 0).sum())
        fixed = max(1, used // 4)
        moved = fixed + (places - fixed + offset_by * (used - fixed)) % max(1, number_of - fixed)
        return jnp.zeros((number_of,), jnp.int32).at[sequence[jnp.where(places < fixed, places, moved)]].set(jnp.asarray(lengths, jnp.int32))

    lengths = jnp.where(number % 4 == 0, named(heavy_load, number // 4), named(common, number - number // 4 - 1))
    mixed = jax.random.permutation(jax.random.fold_in(own, 3), number_of)
    source_of, receiver = mixed[0:number_of // 2 * 2:2], mixed[1:number_of // 2 * 2:2]
    margin = jnp.minimum(lengths[source_of] - 1, reach - lengths[receiver]) // 2
    margin = jnp.where((source_of == sequence[0]) | (receiver == sequence[0]) | (lengths[receiver] == 0), 0, jnp.maximum(margin, 0))
    moved = jax.random.randint(jax.random.fold_in(own, 4), (number_of // 2,), 0, 1 << 20) % (margin + 1)
    lengths = lengths.at[source_of].add(-moved).at[receiver].add(moved)
    members = jnp.searchsorted(jnp.cumsum(lengths), jnp.arange(rows * top), side="right").astype(jnp.int32)
    grid = members.reshape(top, rows).T
    grid = grid[jax.random.permutation(jax.random.fold_in(own, 1), rows)]
    offset_by = jax.random.randint(jax.random.fold_in(own, 2), (rows, 1), 0, top)
    return jnp.take_along_axis(grid, (jnp.arange(top)[None, :] + offset_by) % top, axis=1)


def portions_of(count, total, reach, skew, full):
    weights = [(1 << 20) // math.isqrt(standing ** skew) + 1 for standing in range(1, count + 1)]
    largest = reach if full else min(reach, max(-(-total // count), total * weights[0] // sum(weights)))
    least = 1 if total - largest >= count - 1 else 0
    given, spare = [largest] + [least] * (count - 1), total - largest - least * (count - 1)
    while spare > 0:
        candidates = [i for i in range(1, count) if given[i] < largest] or [i for i in range(1, count) if given[i] < reach]
        whole, remaining = sum([weights[i] for i in candidates]), spare
        for i in candidates:
            extra = min(reach - given[i], max(1, remaining * weights[i] // whole), spare)
            given[i] = given[i] + extra
            spare = spare - extra
    return np.array(given)


def normal_values(key, extent, deviation, most, pieces=(), dtype=jnp.bfloat16):
    factor_of = level_of(key, extent, pieces, -0.22, 0.18) if pieces else 1.0
    entries = jax.random.normal(key, extent, jnp.float32) * deviation * factor_of
    return jnp.minimum(jnp.maximum(entries, -most), most).astype(dtype)


def setup_inputs(seed: int = 0) -> dict:
    seeds = jax.random.split(jax.random.key(seed), 7)
    emitted = normal_values(seeds[0], (N_SECTION, N_PEER, ROWS, D), 1.0, 6.0, ((0, 16), (1, 32)))
    out_grads = normal_values(seeds[1], (N_SECTION, N_PEER, ROWS, D), 1.0, 6.0, ((0, 16), (1, 32)))
    adapter_in = normal_values(seeds[2], (N_SECTION, RANK, D), D ** -0.5, 0.078125, ((0, 16),))
    adapter_out = normal_values(seeds[3], (N_SECTION, RANK, D), 256 ** -0.5, 0.375, ((0, 16),))
    wiring_keys = jax.random.split(jax.random.fold_in(seeds[4], 1), N_SECTION * N_PEER * NB // NB)
    wiring_turns = jax.random.permutation(jax.random.fold_in(seeds[4], 3), N_SECTION * N_PEER * NB // NB)
    wiring = jax.vmap(lambda own, number: assign_block(jax.random.fold_in(seeds[4], 2), own, number, NB, N_PEER, 1, MOST, 0))(wiring_keys, wiring_turns).reshape((N_SECTION, N_PEER, NB, 1))
    counts = with_ends(jax.random.randint(seeds[5], (N_SECTION, N_PEER), 3 * NB // 4, NB + 1), jax.random.fold_in(seeds[5], 1), 3 * NB // 4, NB).astype(jnp.int32)
    return {"emitted": emitted, "out_grads": out_grads, "adapter_in": adapter_in, "adapter_out": adapter_out, "wiring": wiring, "counts": counts}


EPS = 1e-06

def adapter_backward(own_rows, out_rows, row_mask, weight_in, weight_out):
    rows_float = own_rows.astype(jnp.float32)
    inv_rms = lax.rsqrt(lax.optimization_barrier(jnp.mean(rows_float * rows_float, axis=-1, keepdims=True)) + EPS)
    normed_float = rows_float * inv_rms
    normed = normed_float.astype(jnp.bfloat16)
    preact = lax.dot_general(normed, weight_in, (((1,), (1,)), ((), ())), preferred_element_type=jnp.float32)
    activated = jax.nn.silu(preact).astype(jnp.bfloat16)
    masked = (out_rows.astype(jnp.float32) * row_mask).astype(jnp.bfloat16)
    grad_act = lax.dot_general(masked, weight_out, (((1,), (1,)), ((), ())), preferred_element_type=jnp.float32)
    gate_sig = jax.nn.sigmoid(preact)
    grad_pre = (grad_act * gate_sig * (1.0 + preact * (1.0 - gate_sig))).astype(jnp.bfloat16)
    grad_out = lax.dot_general(activated, masked, (((0,), (0,)), ((), ())), preferred_element_type=jnp.float32)
    grad_in = lax.dot_general(grad_pre, normed, (((0,), (0,)), ((), ())), preferred_element_type=jnp.float32)
    grad_norm = jnp.dot(grad_pre, weight_in, preferred_element_type=jnp.float32)
    centred = lax.optimization_barrier(jnp.mean(grad_norm * normed_float, axis=-1, keepdims=True))
    row_grads = masked.astype(jnp.float32) + inv_rms * (grad_norm - normed_float * centred)
    return (row_grads.astype(jnp.bfloat16), grad_in, grad_out)

def reference(emitted, out_grads, adapter_in, adapter_out, wiring, counts):
    targets = wiring[..., 0].astype(jnp.int32)
    order = jnp.arange(NB).astype(jnp.int32)
    matches = targets[..., :, None] == targets[..., None, :]
    earlier = order[None, :] < order[:, None]
    slot_rank = lax.optimization_barrier(jnp.sum(jnp.where(matches & earlier, 1, 0), axis=-1)).astype(jnp.int32)
    active = (order[None, None, :] < counts[..., None]).astype(jnp.float32)
    senders = jnp.arange(N_PEER).astype(jnp.int32)[:, None]
    zero_grad = jnp.zeros((RANK, D), jnp.float32)
    rows_list = []
    in_list = [zero_grad]
    out_list = [zero_grad]
    for section_idx in range(N_SECTION - 1):
        following = section_idx + 1
        incoming = out_grads[following].reshape(N_PEER, N_PEER, MOST, BLK, D)
        paired = incoming[targets[section_idx], senders, slot_rank[section_idx]]
        row_mask = jnp.broadcast_to(active[section_idx][:, :, None], (N_PEER, NB, BLK)).reshape(-1, 1)
        row_grads, grad_in, grad_out = adapter_backward(emitted[section_idx].reshape(-1, D), paired.reshape(-1, D), row_mask, adapter_in[following], adapter_out[following])
        rows_list.append(row_grads.reshape(N_PEER, ROWS, D))
        in_list.append(grad_in / ROWS)
        out_list.append(grad_out / ROWS)
    rows_list.append(jnp.zeros((N_PEER, ROWS, D), jnp.bfloat16))
    return (jnp.stack(rows_list), jnp.stack(in_list), jnp.stack(out_list))
```

```python
import functools

import jax
import jax.numpy as jnp
from jax import lax
from jax.experimental import pallas as pl
from jax.experimental.pallas import tpu as pltpu
from jax.sharding import PartitionSpec as P

EPS = 1e-06
BF16 = jnp.bfloat16
F32 = jnp.float32
LANES = 128
BLK = 4
VMEM = pl.BlockSpec(memory_space=pltpu.VMEM)
SMEM = pl.BlockSpec(memory_space=pltpu.SMEM)
NT = (((1,), (1,)), ((), ()))
TN = (((0,), (0,)), ((), ()))


def params():
    return pltpu.CompilerParams(vmem_limit_bytes=40 * 1024 * 1024)


def cost(flops, moved):
    return pl.CostEstimate(flops=flops, bytes_accessed=moved, transcendentals=0)


def pair_up(first, second):
    upper = lax.broadcasted_iota(jnp.int32, first.shape, first.ndim - 2) < BLK
    axis = first.ndim - 2
    top = jnp.where(upper, first, pltpu.roll(second, BLK, axis))
    bottom = jnp.where(upper, pltpu.roll(first, BLK, axis), second)
    return top, bottom


def pack_kernel(rows_ref, out_ref):
    rows, width = rows_ref.shape
    pairs = rows // 8
    for j in range(0, width // LANES, 4):
        tiles = [
            rows_ref[:, (j + k) * LANES : (j + k + 1) * LANES].astype(F32).reshape(pairs, 8, LANES)
            for k in range(4)
        ]
        even0, odd0 = pair_up(tiles[0], tiles[1])
        even1, odd1 = pair_up(tiles[2], tiles[3])
        even = jnp.concatenate([even0, even1], axis=1)
        odd = jnp.concatenate([odd0, odd1], axis=1)
        blocks = jnp.stack([even, odd], axis=1).reshape(2 * pairs, 16, LANES)
        out_ref[:, 4 * j : 4 * j + 16, :] = blocks.astype(BF16)


def pack(rows):
    count, width = rows.shape
    step = 1024 if width % 1024 == 0 else width
    high = step // LANES * BLK
    return pl.pallas_call(
        pack_kernel,
        grid=(width // step,),
        out_shape=jax.ShapeDtypeStruct((count // BLK, width // LANES * BLK, LANES), BF16),
        in_specs=[pl.BlockSpec((count, step), lambda i: (0, i))],
        out_specs=pl.BlockSpec((count // BLK, high, LANES), lambda i: (0, i, 0)),
        compiler_params=params(),
        cost_estimate=cost(count * width * 8, count * width * 4),
        name="pack_blocks",
    )(rows)


def adapter_kernel(
    meta_ref, blocks_ref, rows_ref, win_ref, wout_ref, grads_ref, sums_ref, masked_ref
):
    blocks = blocks_ref.shape[0]
    rows, width = rows_ref.shape
    tiles = width // LANES
    live_blocks = meta_ref[0, blocks]

    def place(group, _):
        halves = []
        for pair in range(2):
            loaded = []
            for k in range(2):
                b = group * 4 + pair * 2 + k
                live = jnp.where(b < live_blocks, 1.0, 0.0).astype(F32)
                block = blocks_ref[meta_ref[0, b]].astype(F32) * live
                loaded.append(block.reshape(tiles // 2, 8, LANES))
            even, odd = pair_up(loaded[0], loaded[1])
            lanes = []
            for u in range(tiles // 2):
                lanes += [even[u], odd[u]]
            halves.append(jnp.concatenate(lanes, axis=1))
        at = pl.multiple_of(group * 16, 16)
        masked_ref[pl.ds(at, 16), :] = jnp.concatenate(halves, axis=0).astype(BF16)
        return 0

    lax.fori_loop(0, blocks // 4, place, 0)

    squares = jnp.zeros((rows, LANES), F32)
    for j in range(tiles):
        tile = rows_ref[:, j * LANES : (j + 1) * LANES].astype(F32)
        squares += tile * tile
    inv_rms = lax.rsqrt(jnp.sum(squares, axis=1, keepdims=True) * (1.0 / width) + EPS)
    preact = inv_rms * lax.dot_general(
        rows_ref[...], win_ref[...], NT, preferred_element_type=F32
    )
    gate = jax.nn.sigmoid(preact)
    activated = (preact * gate).astype(BF16)
    grad_act = lax.dot_general(
        masked_ref[...], wout_ref[...], NT, preferred_element_type=F32
    )
    grad_pre = grad_act * gate * (1.0 + preact * (1.0 - gate))
    scaled = (grad_pre * inv_rms).astype(BF16)
    coef = inv_rms * jnp.sum(scaled.astype(F32) * preact, axis=1, keepdims=True) * (1.0 / width)

    step = 256
    for j in range(0, width, step):
        here = slice(j, j + step)
        spread = jnp.dot(scaled, win_ref[:, here], preferred_element_type=F32)
        result = masked_ref[:, here].astype(F32) + spread - rows_ref[:, here].astype(F32) * coef
        grads_ref[:, here] = result.astype(BF16)

    grad_in = lax.dot_general(scaled, rows_ref[...], TN, preferred_element_type=F32)
    grad_out = lax.dot_general(activated, masked_ref[...], TN, preferred_element_type=F32)
    store_pieces(sums_ref, grad_in, grad_out)


def store_pieces(sums_ref, grad_in, grad_out):
    per = grad_in.shape[1] // (8 * LANES)
    bands = [grad_in[0:8], grad_in[8:16], grad_out[0:8], grad_out[8:16]]
    for g, band in enumerate(bands):
        for h in range(8):
            for t in range(0, per, 2):
                at = (h * per + t) * LANES
                first = band[:, at : at + LANES]
                second = band[:, at + LANES : at + 2 * LANES] if t + 1 < per else jnp.zeros_like(first)
                both = jnp.concatenate([first, second], axis=0)
                sums_ref[g * 8 + h, 8 * t : 8 * t + 16, :] = both.astype(BF16)


def adapter(meta, blocks, rows, win, wout):
    count, width = rows.shape
    rank = win.shape[0]
    high = -(-width // (8 * LANES) // 2) * 16
    return pl.pallas_call(
        adapter_kernel,
        out_shape=(
            jax.ShapeDtypeStruct((count, width), BF16),
            jax.ShapeDtypeStruct((32, high, LANES), BF16),
        ),
        in_specs=[SMEM, VMEM, VMEM, VMEM, VMEM],
        out_specs=(VMEM, VMEM),
        scratch_shapes=[pltpu.VMEM((count, width), BF16)],
        compiler_params=params(),
        cost_estimate=cost(10 * count * width * rank, count * width * 6),
        name="adapter_backward",
    )(meta, blocks, rows, win, wout)


def sum_kernel(scale, pieces_ref, out_ref):
    total = jnp.sum(pieces_ref[...].astype(F32), axis=0) * scale
    out_ref[...] = jnp.broadcast_to(total.astype(BF16)[None], out_ref.shape)


def sum_pieces(pieces, scale):
    return pl.pallas_call(
        functools.partial(sum_kernel, scale),
        out_shape=jax.ShapeDtypeStruct(pieces.shape, BF16),
        in_specs=[VMEM],
        out_specs=VMEM,
        compiler_params=params(),
        cost_estimate=cost(pieces.size, pieces.size * 4),
        name="sum_pieces",
    )(pieces)


def join_kernel(pieces_ref, in_ref, out_ref):
    per = in_ref.shape[1] // (8 * LANES)
    for g in range(4):
        target = in_ref if g < 2 else out_ref
        rows = slice(8 * (g % 2), 8 * (g % 2) + 8)
        for h in range(8):
            for t in range(0, per, 2):
                at = (h * per + t) * LANES
                both = pieces_ref[g * 8 + h, 8 * t : 8 * t + 16, :].astype(F32)
                target[rows, at : at + LANES] = both[0:8]
                if t + 1 < per:
                    target[rows, at + LANES : at + 2 * LANES] = both[8:16]


def join_pieces(pieces, rank, width):
    return pl.pallas_call(
        join_kernel,
        out_shape=(jax.ShapeDtypeStruct((rank, width), F32),) * 2,
        in_specs=[VMEM],
        out_specs=(VMEM, VMEM),
        compiler_params=params(),
        cost_estimate=cost(pieces.size, pieces.size * 6),
        name="join_pieces",
    )(pieces)


def exchange(pieces):
    return lax.all_to_all(pieces, "peer", split_axis=0, concat_axis=0, tiled=True)


def shards(emitted, out_grads, adapter_in, adapter_out, wiring, counts):
    sections = lax.axis_size("section")
    onward = [(i, (i + 1) % sections) for i in range(sections)]
    back = [((i + 1) % sections, i) for i in range(sections)]
    row_total, width = emitted.shape[2:]
    rank = adapter_in.shape[1]
    last = lax.axis_index("section") == sections - 1

    rows = lax.ppermute(emitted[0, 0], "section", onward)
    live = jnp.where(last, 0, counts)
    meta = jnp.concatenate([wiring[0, 0, :, 0].reshape(1, -1), live], axis=1)
    meta = lax.ppermute(meta, "section", onward)
    blocks = exchange(pack(out_grads[0, 0]))
    grads, sums = adapter(meta, blocks, rows, adapter_in[0], adapter_out[0])
    row_grads = lax.ppermute(grads, "section", back)
    sums = exchange(sum_pieces(exchange(sums), 1.0 / row_total))
    grad_in, grad_out = join_pieces(sums, rank, width)
    return (row_grads[None, None], grad_in[None], grad_out[None])


def solution(mesh):
    return jax.shard_map(
        shards,
        mesh=mesh,
        in_specs=(
            P("section", "peer", None, None),
            P("section", "peer", None, None),
            P("section", None, None),
            P("section", None, None),
            P("section", "peer", None, None),
            P("section", "peer"),
        ),
        out_specs=(
            P("section", "peer", None, None),
            P("section", None, None),
            P("section", None, None),
        ),
        check_vma=False,
    )
```

```python
import functools

import jax
import jax.numpy as jnp
from jax import lax
from jax.experimental import pallas as pl
from jax.experimental.pallas import tpu as pltpu
from jax.sharding import PartitionSpec as P

EPS = 1e-06
BF16 = jnp.bfloat16
F32 = jnp.float32
LANES = 128
BLK = 4
VMEM = pl.BlockSpec(memory_space=pltpu.VMEM)
SMEM = pl.BlockSpec(memory_space=pltpu.SMEM)
NT = (((1,), (1,)), ((), ()))
TN = (((0,), (0,)), ((), ()))


def params():
    return pltpu.CompilerParams(vmem_limit_bytes=40 * 1024 * 1024)


def cost(flops, moved):
    return pl.CostEstimate(flops=flops, bytes_accessed=moved, transcendentals=0)


def pair_up(first, second):
    upper = lax.broadcasted_iota(jnp.int32, first.shape, first.ndim - 2) < BLK
    axis = first.ndim - 2
    top = jnp.where(upper, first, pltpu.roll(second, BLK, axis))
    bottom = jnp.where(upper, pltpu.roll(first, BLK, axis), second)
    return top, bottom


def pack_kernel(rows_ref, out_ref):
    rows, width = rows_ref.shape
    pairs = rows // 8
    for j in range(0, width // LANES, 4):
        tiles = [
            rows_ref[:, (j + k) * LANES : (j + k + 1) * LANES].astype(F32).reshape(pairs, 8, LANES)
            for k in range(4)
        ]
        even0, odd0 = pair_up(tiles[0], tiles[1])
        even1, odd1 = pair_up(tiles[2], tiles[3])
        even = jnp.concatenate([even0, even1], axis=1)
        odd = jnp.concatenate([odd0, odd1], axis=1)
        blocks = jnp.stack([even, odd], axis=1).reshape(2 * pairs, 16, LANES)
        out_ref[:, 4 * j : 4 * j + 16, :] = blocks.astype(BF16)


def pack(rows):
    count, width = rows.shape
    step = 1024 if width % 1024 == 0 else width
    high = step // LANES * BLK
    return pl.pallas_call(
        pack_kernel,
        grid=(width // step,),
        out_shape=jax.ShapeDtypeStruct((count // BLK, width // LANES * BLK, LANES), BF16),
        in_specs=[pl.BlockSpec((count, step), lambda i: (0, i))],
        out_specs=pl.BlockSpec((count // BLK, high, LANES), lambda i: (0, i, 0)),
        compiler_params=params(),
        cost_estimate=cost(count * width * 8, count * width * 4),
        name="pack_blocks",
    )(rows)


def adapter_kernel(
    meta_ref, blocks_ref, rows_ref, win_ref, wout_ref, grads_ref, sums_ref, masked_ref
):
    blocks = blocks_ref.shape[0]
    rows, width = rows_ref.shape
    tiles = width // LANES
    live_blocks = meta_ref[0, blocks]

    def place(group, _):
        halves = []
        for pair in range(2):
            loaded = []
            for k in range(2):
                b = group * 4 + pair * 2 + k
                live = jnp.where(b < live_blocks, 1.0, 0.0).astype(F32)
                block = blocks_ref[meta_ref[0, b]].astype(F32) * live
                loaded.append(block.reshape(tiles // 2, 8, LANES))
            even, odd = pair_up(loaded[0], loaded[1])
            lanes = []
            for u in range(tiles // 2):
                lanes += [even[u], odd[u]]
            halves.append(jnp.concatenate(lanes, axis=1))
        at = pl.multiple_of(group * 16, 16)
        masked_ref[pl.ds(at, 16), :] = jnp.concatenate(halves, axis=0).astype(BF16)
        return 0

    lax.fori_loop(0, blocks // 4, place, 0)

    squares = jnp.zeros((rows, LANES), F32)
    for j in range(tiles):
        tile = rows_ref[:, j * LANES : (j + 1) * LANES].astype(F32)
        squares += tile * tile
    inv_rms = lax.rsqrt(jnp.sum(squares, axis=1, keepdims=True) * (1.0 / width) + EPS)
    preact = inv_rms * lax.dot_general(
        rows_ref[...], win_ref[...], NT, preferred_element_type=F32
    )
    gate = jax.nn.sigmoid(preact)
    activated = (preact * gate).astype(BF16)
    grad_act = lax.dot_general(
        masked_ref[...], wout_ref[...], NT, preferred_element_type=F32
    )
    grad_pre = grad_act * gate * (1.0 + preact * (1.0 - gate))
    scaled = (grad_pre * inv_rms).astype(BF16)
    coef = inv_rms * jnp.sum(scaled.astype(F32) * preact, axis=1, keepdims=True) * (1.0 / width)

    step = 256
    for j in range(0, width, step):
        here = slice(j, j + step)
        spread = jnp.dot(scaled, win_ref[:, here], preferred_element_type=F32)
        result = masked_ref[:, here].astype(F32) + spread - rows_ref[:, here].astype(F32) * coef
        grads_ref[:, here] = result.astype(BF16)

    grad_in = lax.dot_general(scaled, rows_ref[...], TN, preferred_element_type=F32)
    grad_out = lax.dot_general(activated, masked_ref[...], TN, preferred_element_type=F32)
    store_pieces(sums_ref, grad_in, grad_out)


def store_pieces(sums_ref, grad_in, grad_out):
    span = sums_ref.shape[2]
    bands = [grad_in[0:8], grad_in[8:16], grad_out[0:8], grad_out[8:16]]
    for g, band in enumerate(bands):
        for h in range(8):
            sums_ref[g * 8 + h] = band[:, h * span : (h + 1) * span].astype(BF16)


def adapter(meta, blocks, rows, win, wout):
    count, width = rows.shape
    rank = win.shape[0]
    return pl.pallas_call(
        adapter_kernel,
        out_shape=(
            jax.ShapeDtypeStruct((count, width), BF16),
            jax.ShapeDtypeStruct((32, 8, width // 8), BF16),
        ),
        in_specs=[SMEM, VMEM, VMEM, VMEM, VMEM],
        out_specs=(VMEM, VMEM),
        scratch_shapes=[pltpu.VMEM((count, width), BF16)],
        compiler_params=params(),
        cost_estimate=cost(10 * count * width * rank, count * width * 6),
        name="adapter_backward",
    )(meta, blocks, rows, win, wout)


def sum_kernel(scale, pieces_ref, out_ref):
    total = jnp.sum(pieces_ref[...].astype(F32), axis=0) * scale
    out_ref[...] = jnp.broadcast_to(total.astype(BF16)[None], out_ref.shape)


def sum_pieces(pieces, scale):
    return pl.pallas_call(
        functools.partial(sum_kernel, scale),
        out_shape=jax.ShapeDtypeStruct(pieces.shape, BF16),
        in_specs=[VMEM],
        out_specs=VMEM,
        compiler_params=params(),
        cost_estimate=cost(pieces.size, pieces.size * 4),
        name="sum_pieces",
    )(pieces)


def join_kernel(pieces_ref, in_ref, out_ref):
    span = pieces_ref.shape[2]
    for g in range(4):
        target = in_ref if g < 2 else out_ref
        rows = slice(8 * (g % 2), 8 * (g % 2) + 8)
        for h in range(8):
            target[rows, h * span : (h + 1) * span] = pieces_ref[g * 8 + h].astype(F32)


def join_pieces(pieces, rank, width):
    return pl.pallas_call(
        join_kernel,
        out_shape=(jax.ShapeDtypeStruct((rank, width), F32),) * 2,
        in_specs=[VMEM],
        out_specs=(VMEM, VMEM),
        compiler_params=params(),
        cost_estimate=cost(pieces.size, pieces.size * 6),
        name="join_pieces",
    )(pieces)


def exchange(pieces):
    return lax.all_to_all(pieces, "peer", split_axis=0, concat_axis=0, tiled=True)


def shards(emitted, out_grads, adapter_in, adapter_out, wiring, counts):
    sections = lax.axis_size("section")
    onward = [(i, i + 1) for i in range(sections - 1)]
    back = [(i + 1, i) for i in range(sections - 1)]
    row_total, width = emitted.shape[2:]
    rank = adapter_in.shape[1]

    rows = lax.ppermute(emitted[0, 0], "section", onward)
    meta = jnp.concatenate([wiring[0, 0, :, 0].reshape(1, -1), counts], axis=1)
    meta = lax.ppermute(meta, "section", onward)
    blocks = exchange(pack(out_grads[0, 0]))
    grads, sums = adapter(meta, blocks, rows, adapter_in[0], adapter_out[0])
    row_grads = lax.ppermute(grads, "section", back)
    sums = exchange(sum_pieces(exchange(sums), 1.0 / row_total))
    grad_in, grad_out = join_pieces(sums, rank, width)
    return (row_grads[None, None], grad_in[None], grad_out[None])


def solution(mesh):
    return jax.shard_map(
        shards,
        mesh=mesh,
        in_specs=(
            P("section", "peer", None, None),
            P("section", "peer", None, None),
            P("section", None, None),
            P("section", None, None),
            P("section", "peer", None, None),
            P("section", "peer"),
        ),
        out_specs=(
            P("section", "peer", None, None),
            P("section", None, None),
            P("section", None, None),
        ),
        check_vma=False,
    )
```

```python
import functools

import jax
import jax.numpy as jnp
from jax import lax
from jax.experimental import pallas as pl
from jax.experimental.pallas import tpu as pltpu
from jax.sharding import PartitionSpec as P

EPS = 1e-06
BF16 = jnp.bfloat16
F32 = jnp.float32
LANES = 128
BLK = 4
VMEM = pl.BlockSpec(memory_space=pltpu.VMEM)
SMEM = pl.BlockSpec(memory_space=pltpu.SMEM)
ANY = pl.BlockSpec(memory_space=pl.ANY)
CHUNK = 1024
PACK_LIMIT = 62 * 1024 * 1024
NT = (((1,), (1,)), ((), ()))
TN = (((0,), (0,)), ((), ()))


def params():
    return pltpu.CompilerParams(vmem_limit_bytes=40 * 1024 * 1024)


def cost(flops, moved):
    return pl.CostEstimate(flops=flops, bytes_accessed=moved, transcendentals=0)


def pair_up(first, second):
    upper = lax.broadcasted_iota(jnp.int32, first.shape, first.ndim - 2) < BLK
    axis = first.ndim - 2
    top = jnp.where(upper, first, pltpu.roll(second, BLK, axis))
    bottom = jnp.where(upper, pltpu.roll(first, BLK, axis), second)
    return top, bottom


def pack_kernel(chunk, rows_ref, out_ref, rows_buf, out_buf, in_sem, out_sem):
    rows, width = rows_buf.shape
    pairs = rows // 8
    high = chunk // LANES * BLK

    def load(c):
        here = slice(c * chunk, (c + 1) * chunk)
        return pltpu.make_async_copy(rows_ref.at[:, here], rows_buf.at[:, here], in_sem.at[c])

    def save(c):
        here = slice(c * high, (c + 1) * high)
        return pltpu.make_async_copy(out_buf.at[:, here], out_ref.at[:, here], out_sem.at[c])

    for c in range(width // chunk):
        load(c).start()
    for c in range(width // chunk):
        load(c).wait()
        for j in range(c * chunk // LANES, (c + 1) * chunk // LANES, 4):
            tiles = [
                rows_buf[:, (j + k) * LANES : (j + k + 1) * LANES]
                .astype(F32)
                .reshape(pairs, 8, LANES)
                for k in range(4)
            ]
            even0, odd0 = pair_up(tiles[0], tiles[1])
            even1, odd1 = pair_up(tiles[2], tiles[3])
            even = jnp.concatenate([even0, even1], axis=1)
            odd = jnp.concatenate([odd0, odd1], axis=1)
            blocks = jnp.stack([even, odd], axis=1).reshape(2 * pairs, 16, LANES)
            out_buf[:, 4 * j : 4 * j + 16, :] = blocks.astype(BF16)
        save(c).start()
    for c in range(width // chunk):
        save(c).wait()


def pack(rows):
    count, width = rows.shape
    chunk = CHUNK if width % CHUNK == 0 else width
    shape = (count // BLK, width // LANES * BLK, LANES)
    return pl.pallas_call(
        functools.partial(pack_kernel, chunk),
        out_shape=jax.ShapeDtypeStruct(shape, BF16),
        in_specs=[ANY],
        out_specs=ANY,
        scratch_shapes=[
            pltpu.VMEM((count, width), BF16),
            pltpu.VMEM(shape, BF16),
            pltpu.SemaphoreType.DMA((width // chunk,)),
            pltpu.SemaphoreType.DMA((width // chunk,)),
        ],
        compiler_params=pltpu.CompilerParams(vmem_limit_bytes=PACK_LIMIT),
        cost_estimate=cost(count * width * 8, count * width * 4),
        name="pack_blocks",
    )(rows)


def place_blocks(meta_ref, blocks_ref, rows_ref):
    blocks = blocks_ref.shape[0]
    tiles = rows_ref.shape[1] // LANES

    def place(group):
        halves = []
        for pair in range(2):
            loaded = []
            for k in range(2):
                b = group * 4 + pair * 2 + k
                block = blocks_ref[meta_ref[0, b]].astype(F32)
                loaded.append(block.reshape(tiles // 2, 8, LANES))
            even, odd = pair_up(loaded[0], loaded[1])
            lanes = []
            for u in range(tiles // 2):
                lanes += [even[u], odd[u]]
            halves.append(jnp.concatenate(lanes, axis=1))
        rows_ref[group * 16 : group * 16 + 16, :] = jnp.concatenate(halves, axis=0).astype(BF16)

    for group in range(blocks // 4):
        place(group)


def live_rows(meta_ref, blocks, rows):
    row = lax.broadcasted_iota(jnp.int32, (rows, 1), 0)
    return jnp.where(row < meta_ref[0, blocks] * BLK, 1.0, 0.0).astype(F32)


def adapter_kernel(
    meta_ref, blocks_ref, rows_ref, win_ref, wout_ref, grads_ref, pre_ref, act_ref, paired_ref, normed_ref
):
    rows, width = rows_ref.shape
    rank = win_ref.shape[0]
    tiles = width // LANES
    live = live_rows(meta_ref, blocks_ref.shape[0], rows)
    totals = jnp.zeros((rows, LANES), F32)
    for j in range(tiles):
        tile = rows_ref[:, j * LANES : (j + 1) * LANES].astype(F32)
        totals += tile * tile
    squares = jnp.sum(totals, axis=1, keepdims=True)
    inv_rms = lax.rsqrt(squares * (1.0 / width) + EPS)
    place_blocks(meta_ref, blocks_ref, paired_ref)
    for j in range(tiles):
        here = slice(j * LANES, (j + 1) * LANES)
        normed_ref[:, here] = (rows_ref[:, here].astype(F32) * inv_rms).astype(BF16)
    grad_act = live * lax.dot_general(
        paired_ref[...], wout_ref[...], NT, preferred_element_type=F32
    )
    preact = lax.dot_general(win_ref[...], normed_ref[...], NT, preferred_element_type=F32).T
    gate = jax.nn.sigmoid(preact)
    activated = (live * (preact * gate)).astype(BF16)
    grad_pre = (grad_act * gate * (1.0 + preact * (1.0 - gate))).astype(BF16)
    pre_ref[...] = grad_pre
    act_ref[...] = activated
    centred = jnp.sum(grad_pre.astype(F32) * preact, axis=1, keepdims=True) * (1.0 / width)
    coef = inv_rms * inv_rms * centred
    step = 256
    for j in range(0, width, step):
        here = slice(j, j + step)
        spread = jnp.dot(grad_pre, win_ref[:, here], preferred_element_type=F32)
        result = paired_ref[:, here].astype(F32) * live + (
            inv_rms * spread - rows_ref[:, here].astype(F32) * coef
        )
        grads_ref[:, here] = result.astype(BF16)


def sums_kernel(pre_ref, act_ref, paired_ref, normed_ref, sums_ref):
    grad_in = lax.dot_general(pre_ref[...], normed_ref[...], TN, preferred_element_type=F32)
    grad_out = lax.dot_general(act_ref[...], paired_ref[...], TN, preferred_element_type=F32)
    store_pieces(sums_ref, grad_in, grad_out)


def store_pieces(sums_ref, grad_in, grad_out):
    span = sums_ref.shape[2]
    bands = [grad_in[0:8], grad_in[8:16], grad_out[0:8], grad_out[8:16]]
    for g, band in enumerate(bands):
        for h in range(8):
            sums_ref[g * 8 + h] = band[:, h * span : (h + 1) * span].astype(BF16)


def adapter(meta, blocks, rows, win, wout):
    count, width = rows.shape
    rank = win.shape[0]
    wide = jax.ShapeDtypeStruct((count, width), BF16)
    narrow = jax.ShapeDtypeStruct((count, rank), BF16)
    return pl.pallas_call(
        adapter_kernel,
        out_shape=(wide, narrow, narrow, wide, wide),
        in_specs=[SMEM, VMEM, VMEM, VMEM, VMEM],
        out_specs=(VMEM,) * 5,
        compiler_params=params(),
        cost_estimate=cost(6 * count * width * rank, count * width * 10),
        name="row_grads",
    )(meta, blocks, rows, win, wout)


def local_sums(pre, act, paired, normed):
    count, width = paired.shape
    return pl.pallas_call(
        sums_kernel,
        out_shape=jax.ShapeDtypeStruct((32, 8, width // 8), BF16),
        in_specs=[VMEM] * 4,
        out_specs=VMEM,
        compiler_params=params(),
        cost_estimate=cost(4 * count * width * act.shape[1], count * width * 4),
        name="local_sums",
    )(pre, act, paired, normed)


def sum_kernel(scale, pieces_ref, out_ref):
    total = jnp.sum(pieces_ref[...].astype(F32), axis=0) * scale
    out_ref[...] = jnp.broadcast_to(total.astype(BF16)[None], out_ref.shape)


def sum_pieces(pieces, scale):
    return pl.pallas_call(
        functools.partial(sum_kernel, scale),
        out_shape=jax.ShapeDtypeStruct(pieces.shape, BF16),
        in_specs=[VMEM],
        out_specs=VMEM,
        compiler_params=params(),
        cost_estimate=cost(pieces.size, pieces.size * 4),
        name="sum_pieces",
    )(pieces)


def join_kernel(pieces_ref, in_ref, out_ref):
    span = pieces_ref.shape[2]
    for g in range(4):
        target = in_ref if g < 2 else out_ref
        rows = slice(8 * (g % 2), 8 * (g % 2) + 8)
        for h in range(8):
            target[rows, h * span : (h + 1) * span] = pieces_ref[g * 8 + h].astype(F32)


def join_pieces(pieces, rank, width):
    return pl.pallas_call(
        join_kernel,
        out_shape=(jax.ShapeDtypeStruct((rank, width), F32),) * 2,
        in_specs=[VMEM],
        out_specs=(VMEM, VMEM),
        compiler_params=params(),
        cost_estimate=cost(pieces.size, pieces.size * 6),
        name="join_pieces",
    )(pieces)


def exchange(pieces):
    return lax.all_to_all(pieces, "peer", split_axis=0, concat_axis=0, tiled=True)


def shards(emitted, out_grads, adapter_in, adapter_out, wiring, counts):
    sections = lax.axis_size("section")
    onward = [(i, i + 1) for i in range(sections - 1)]
    back = [(i + 1, i) for i in range(sections - 1)]
    row_total, width = emitted.shape[2:]
    rank = adapter_in.shape[1]

    rows = lax.ppermute(emitted[0, 0], "section", onward)
    meta = jnp.concatenate([wiring[0, 0, :, 0].reshape(1, -1), counts], axis=1)
    meta = lax.ppermute(meta, "section", onward)
    blocks = exchange(pack(out_grads[0, 0]))
    grads, *factors = adapter(meta, blocks, rows, adapter_in[0], adapter_out[0])
    row_grads = lax.ppermute(grads, "section", back)
    sums = local_sums(*factors)
    sums = exchange(sum_pieces(exchange(sums), 1.0 / row_total))
    grad_in, grad_out = join_pieces(sums, rank, width)
    return (row_grads[None, None], grad_in[None], grad_out[None])


def solution(mesh):
    return jax.shard_map(
        shards,
        mesh=mesh,
        in_specs=(
            P("section", "peer", None, None),
            P("section", "peer", None, None),
            P("section", None, None),
            P("section", None, None),
            P("section", "peer", None, None),
            P("section", "peer"),
        ),
        out_specs=(
            P("section", "peer", None, None),
            P("section", None, None),
            P("section", None, None),
        ),
        check_vma=False,
    )
```

```python
import functools

import jax
import jax.numpy as jnp
from jax import lax
from jax.experimental import pallas as pl
from jax.experimental.pallas import tpu as pltpu
from jax.sharding import PartitionSpec as P

EPS = 1e-06
BF16 = jnp.bfloat16
F32 = jnp.float32
LANES = 128
BLK = 4
VMEM = pl.BlockSpec(memory_space=pltpu.VMEM)
SMEM = pl.BlockSpec(memory_space=pltpu.SMEM)
ANY = pl.BlockSpec(memory_space=pl.ANY)
CHUNK = 1024
PACK_LIMIT = 60 * 1024 * 1024
NT = (((1,), (1,)), ((), ()))
TN = (((0,), (0,)), ((), ()))


def params():
    return pltpu.CompilerParams(vmem_limit_bytes=40 * 1024 * 1024)


def cost(flops, moved):
    return pl.CostEstimate(flops=flops, bytes_accessed=moved, transcendentals=0)


def old(flops, moved):
    return pl.CostEstimate(flops=flops, bytes_accessed=moved, transcendentals=0)


def pair_up(first, second):
    upper = lax.broadcasted_iota(jnp.int32, first.shape, first.ndim - 2) < BLK
    axis = first.ndim - 2
    top = jnp.where(upper, first, pltpu.roll(second, BLK, axis))
    bottom = jnp.where(upper, pltpu.roll(first, BLK, axis), second)
    return top, bottom


def pack_kernel(chunk, rows_ref, out_ref, rows_buf, out_buf, in_sem, out_sem):
    rows, width = rows_buf.shape
    pairs = rows // 8
    high = chunk // LANES * BLK

    def load(c):
        here = slice(c * chunk, (c + 1) * chunk)
        return pltpu.make_async_copy(rows_ref.at[:, here], rows_buf.at[:, here], in_sem.at[c])

    def save(c):
        here = slice(c * high, (c + 1) * high)
        return pltpu.make_async_copy(out_buf.at[:, here], out_ref.at[:, here], out_sem.at[c])

    for c in range(width // chunk):
        load(c).start()
    for c in range(width // chunk):
        load(c).wait()
        for j in range(c * chunk // LANES, (c + 1) * chunk // LANES, 4):
            tiles = [
                rows_buf[:, (j + k) * LANES : (j + k + 1) * LANES]
                .astype(F32)
                .reshape(pairs, 8, LANES)
                for k in range(4)
            ]
            even0, odd0 = pair_up(tiles[0], tiles[1])
            even1, odd1 = pair_up(tiles[2], tiles[3])
            even = jnp.concatenate([even0, even1], axis=1)
            odd = jnp.concatenate([odd0, odd1], axis=1)
            blocks = jnp.stack([even, odd], axis=1).reshape(2 * pairs, 16, LANES)
            out_buf[:, 4 * j : 4 * j + 16, :] = blocks.astype(BF16)
        save(c).start()
    for c in range(width // chunk):
        save(c).wait()


def pack(rows):
    count, width = rows.shape
    chunk = CHUNK if width % CHUNK == 0 else width
    shape = (count // BLK, width // LANES * BLK, LANES)
    return pl.pallas_call(
        functools.partial(pack_kernel, chunk),
        out_shape=jax.ShapeDtypeStruct(shape, BF16),
        in_specs=[ANY],
        out_specs=ANY,
        scratch_shapes=[
            pltpu.VMEM((count, width), BF16),
            pltpu.VMEM(shape, BF16),
            pltpu.SemaphoreType.DMA((width // chunk,)),
            pltpu.SemaphoreType.DMA((width // chunk,)),
        ],
        compiler_params=pltpu.CompilerParams(vmem_limit_bytes=PACK_LIMIT),
        cost_estimate=cost(count * width * 8, count * width * 4),
        name="pack_blocks",
    )(rows)


def place_blocks(meta_ref, blocks_ref, rows_ref):
    blocks = blocks_ref.shape[0]
    tiles = rows_ref.shape[1] // LANES

    def place(group):
        halves = []
        for pair in range(2):
            loaded = []
            for k in range(2):
                b = group * 4 + pair * 2 + k
                block = blocks_ref[meta_ref[0, b]].astype(F32)
                loaded.append(block.reshape(tiles // 2, 8, LANES))
            even, odd = pair_up(loaded[0], loaded[1])
            lanes = []
            for u in range(tiles // 2):
                lanes += [even[u], odd[u]]
            halves.append(jnp.concatenate(lanes, axis=1))
        rows_ref[group * 16 : group * 16 + 16, :] = jnp.concatenate(halves, axis=0).astype(BF16)

    for group in range(blocks // 4):
        place(group)


def live_rows(meta_ref, blocks, rows):
    row = lax.broadcasted_iota(jnp.int32, (rows, 1), 0)
    return jnp.where(row < meta_ref[0, blocks] * BLK, 1.0, 0.0).astype(F32)


def adapter_kernel(
    meta_ref, blocks_ref, rows_ref, win_ref, wout_ref, sums_ref, paired_ref, normed_ref
):
    rows, width = rows_ref.shape
    rank = win_ref.shape[0]
    tiles = width // LANES
    live = live_rows(meta_ref, blocks_ref.shape[0], rows)
    totals = jnp.zeros((rows, LANES), F32)
    for j in range(tiles):
        tile = rows_ref[:, j * LANES : (j + 1) * LANES].astype(F32)
        totals += tile * tile
    squares = jnp.sum(totals, axis=1, keepdims=True)
    inv_rms = lax.rsqrt(squares * (1.0 / width) + EPS)
    place_blocks(meta_ref, blocks_ref, paired_ref)
    for j in range(tiles):
        here = slice(j * LANES, (j + 1) * LANES)
        normed_ref[:, here] = (rows_ref[:, here].astype(F32) * inv_rms).astype(BF16)
    grad_act = live * lax.dot_general(
        paired_ref[...], wout_ref[...], NT, preferred_element_type=F32
    )
    preact = lax.dot_general(win_ref[...], normed_ref[...], NT, preferred_element_type=F32).T
    gate = jax.nn.sigmoid(preact)
    activated = (live * (preact * gate)).astype(BF16)
    grad_pre = (grad_act * gate * (1.0 + preact * (1.0 - gate))).astype(BF16)
    grad_in = lax.dot_general(grad_pre, normed_ref[...], TN, preferred_element_type=F32)
    grad_out = lax.dot_general(activated, paired_ref[...], TN, preferred_element_type=F32)
    store_pieces(sums_ref, grad_in, grad_out)


def store_pieces(sums_ref, grad_in, grad_out):
    span = sums_ref.shape[2]
    bands = [grad_in[0:8], grad_in[8:16], grad_out[0:8], grad_out[8:16]]
    for g, band in enumerate(bands):
        for h in range(8):
            sums_ref[g * 8 + h] = band[:, h * span : (h + 1) * span].astype(BF16)


def adapter(meta, blocks, rows, win, wout):
    count, width = rows.shape
    return pl.pallas_call(
        adapter_kernel,
        out_shape=jax.ShapeDtypeStruct((32, 8, width // 8), BF16),
        in_specs=[SMEM, VMEM, VMEM, VMEM, VMEM],
        out_specs=VMEM,
        scratch_shapes=[pltpu.VMEM((count, width), BF16), pltpu.VMEM((count, width), BF16)],
        compiler_params=params(),
        cost_estimate=cost(100_000_000_000, 200_000_000),
        name="adapter_backward",
    )(meta, blocks, rows, win, wout)


def norm_kernel(rows_ref, win_ref, inv_ref, preact_ref, normed_ref):
    rows, width = rows_ref.shape
    tiles = width // LANES
    totals = jnp.zeros((rows, LANES), F32)
    for j in range(tiles):
        tile = rows_ref[:, j * LANES : (j + 1) * LANES].astype(F32)
        totals += tile * tile
    squares = jnp.sum(totals, axis=1, keepdims=True)
    inv_rms = lax.rsqrt(squares * (1.0 / width) + EPS)
    for j in range(tiles):
        here = slice(j * LANES, (j + 1) * LANES)
        normed_ref[:, here] = (rows_ref[:, here].astype(F32) * inv_rms).astype(BF16)
    inv_ref[...] = inv_rms
    preact_ref[...] = lax.dot_general(
        normed_ref[...], win_ref[...], NT, preferred_element_type=F32
    )


def norm(rows, win):
    count, width = rows.shape
    rank = win.shape[0]
    return pl.pallas_call(
        norm_kernel,
        out_shape=(
            jax.ShapeDtypeStruct((count, 1), F32),
            jax.ShapeDtypeStruct((count, rank), F32),
        ),
        in_specs=[VMEM, VMEM],
        out_specs=(VMEM, VMEM),
        scratch_shapes=[pltpu.VMEM((count, width), BF16)],
        compiler_params=params(),
        cost_estimate=cost(2 * count * width * rank, count * width * 2),
        name="norm_rows",
    )(rows, win)


def finish_kernel(
    meta_ref, blocks_ref, rows_ref, win_ref, wout_ref, inv_ref, preact_ref,
    out_ref, paired_ref, out_buf, out_sem,
):
    rows, width = rows_ref.shape
    live = live_rows(meta_ref, blocks_ref.shape[0], rows)
    inv_rms = inv_ref[...]
    preact = preact_ref[...]
    gate = jax.nn.sigmoid(preact)
    place_blocks(meta_ref, blocks_ref, paired_ref)
    grad_act = live * lax.dot_general(
        paired_ref[...], wout_ref[...], NT, preferred_element_type=F32
    )
    grad_pre = (grad_act * gate * (1.0 + preact * (1.0 - gate))).astype(BF16)
    centred = jnp.sum(grad_pre.astype(F32) * preact, axis=1, keepdims=True) * (1.0 / width)
    coef = inv_rms * inv_rms * centred

    step = 256
    per = 4 * step
    for j in range(0, width, step):
        here = slice(j, j + step)
        spread = jnp.dot(grad_pre, win_ref[:, here], preferred_element_type=F32)
        result = paired_ref[:, here].astype(F32) * live + (
            inv_rms * spread - rows_ref[:, here].astype(F32) * coef
        )
        out_buf[:, here] = result.astype(BF16)
        if (j + step) % per == 0:
            save(out_buf, out_ref, out_sem, per, j // per).start()
    for c in range(width // per):
        save(out_buf, out_ref, out_sem, per, c).wait()


def save(out_buf, out_ref, out_sem, per, c):
    part = slice(c * per, (c + 1) * per)
    return pltpu.make_async_copy(out_buf.at[:, part], out_ref.at[:, part], out_sem.at[c])


def finish(meta, blocks, rows, win, wout, inv_rms, preact):
    count, width = rows.shape
    rank = win.shape[0]
    return pl.pallas_call(
        finish_kernel,
        out_shape=jax.ShapeDtypeStruct((count, width), BF16),
        in_specs=[SMEM] + [VMEM] * 6,
        out_specs=ANY,
        scratch_shapes=[
            pltpu.VMEM((count, width), BF16),
            pltpu.VMEM((count, width), BF16),
            pltpu.SemaphoreType.DMA((width // 1024,)),
        ],
        compiler_params=params(),
        cost_estimate=cost(2 * count * width * rank, count * width * 4),
        name="row_grads",
    )(meta, blocks, rows, win, wout, inv_rms, preact)


def sum_kernel(scale, pieces_ref, out_ref):
    total = jnp.sum(pieces_ref[...].astype(F32), axis=0) * scale
    out_ref[...] = jnp.broadcast_to(total.astype(BF16)[None], out_ref.shape)


def sum_pieces(pieces, scale):
    return pl.pallas_call(
        functools.partial(sum_kernel, scale),
        out_shape=jax.ShapeDtypeStruct(pieces.shape, BF16),
        in_specs=[VMEM],
        out_specs=VMEM,
        compiler_params=params(),
        cost_estimate=cost(pieces.size, pieces.size * 4),
        name="sum_pieces",
    )(pieces)


def join_kernel(pieces_ref, in_ref, out_ref):
    span = pieces_ref.shape[2]
    for g in range(4):
        target = in_ref if g < 2 else out_ref
        rows = slice(8 * (g % 2), 8 * (g % 2) + 8)
        for h in range(8):
            target[rows, h * span : (h + 1) * span] = pieces_ref[g * 8 + h].astype(F32)


def join_pieces(pieces, rank, width):
    return pl.pallas_call(
        join_kernel,
        out_shape=(jax.ShapeDtypeStruct((rank, width), F32),) * 2,
        in_specs=[VMEM],
        out_specs=(VMEM, VMEM),
        compiler_params=params(),
        cost_estimate=cost(pieces.size, pieces.size * 6),
        name="join_pieces",
    )(pieces)


def exchange(pieces):
    return lax.all_to_all(pieces, "peer", split_axis=0, concat_axis=0, tiled=True)


def shards(emitted, out_grads, adapter_in, adapter_out, wiring, counts):
    sections = lax.axis_size("section")
    onward = [(i, i + 1) for i in range(sections - 1)]
    back = [(i + 1, i) for i in range(sections - 1)]
    row_total, width = emitted.shape[2:]
    rank = adapter_in.shape[1]

    rows = lax.ppermute(emitted[0, 0], "section", onward)
    own_meta = jnp.concatenate([wiring[0, 0, :, 0].reshape(1, -1), counts], axis=1)
    meta = lax.ppermute(own_meta, "section", onward)
    next_win = lax.ppermute(adapter_in[0], "section", back)
    next_wout = lax.ppermute(adapter_out[0], "section", back)
    inv_rms, preact = norm(emitted[0, 0], next_win)
    blocks = exchange(pack(out_grads[0, 0]))
    blocks, next_win, next_wout, inv_rms, preact = lax.optimization_barrier(
        (blocks, next_win, next_wout, inv_rms, preact)
    )
    returned = lax.ppermute(blocks, "section", back)
    sums = adapter(meta, blocks, rows, adapter_in[0], adapter_out[0])
    sums = exchange(sum_pieces(exchange(sums), 1.0 / row_total))
    grad_in, grad_out = join_pieces(sums, rank, width)
    grad_in, grad_out, returned = lax.optimization_barrier((grad_in, grad_out, returned))
    row_grads = finish(own_meta, returned, emitted[0, 0], next_win, next_wout, inv_rms, preact)
    return (row_grads[None, None], grad_in[None], grad_out[None])


def solution(mesh):
    return jax.shard_map(
        shards,
        mesh=mesh,
        in_specs=(
            P("section", "peer", None, None),
            P("section", "peer", None, None),
            P("section", None, None),
            P("section", None, None),
            P("section", "peer", None, None),
            P("section", "peer"),
        ),
        out_specs=(
            P("section", "peer", None, None),
            P("section", None, None),
            P("section", None, None),
        ),
        check_vma=False,
    )
```
